32 devices in a mesh: gx: 4 (over y, core), gy: 8 (over z, x).
Axes of the slice: x: 2, y: 2, z: 4, core: 2. Of those that a mesh axis runs over, the one named last changes fastest.
Arguments:
- model_state: float32 [200, 128, 1024], P(None, 'gx', 'gy'), may hold values from -6 to 6
- obs_cell: int32 [32, 2048], P(('gx', 'gy')), may hold values from 0 to 4095
- obs_count: int32 [32, 32], P(('gx', 'gy')), may hold values from 0 to 64, as said below
- obs_value: float32 [16, 65536], P(None, ('gx', 'gy')), may hold values from -6 to 6
- obs_weight: float32 [16, 65536], P(None, ('gx', 'gy')), may hold values from 0.25 to 4
- predictor: float32 [8, 65536], P(None, ('gx', 'gy')), may hold values from -6 to 6
- bias_coef: float32 [16, 8], replicated, may hold values from -3 to 3
- weight_in: float32 [768, 200], replicated, may hold values from -0.4375 to 0.4375
- bias_in: float32 [768], replicated, may hold values from -3 to 3
- weight_mid: float32 [768, 768], replicated, may hold values from -0.21875 to 0.21875
- bias_mid: float32 [768], replicated, may hold values from -3 to 3
- weight_out: float32 [16, 768], replicated, may hold values from -0.21875 to 0.21875
- bias_out: float32 [16], replicated, may hold values from -4 to 4
Outputs:
- gradient: float32 [200, 128, 1024], P(None, 'gx', 'gy')
- evolved: float32 [16, 65536], P(None, ('gx', 'gy'))
- bias_gradient: float32 [16, 8], replicated
The draws below stay inside these ranges and needn't reach their ends.
Inputs may be any that keep to these rules, and one draw needn't show every extreme that they name: obs_count[o, s] is how many of the 64 slots that owner o keeps for grid block s are used, from the first on; for some block s every owner uses all 64. `obs_cell`: a cell within a block is numbered row within the block times 128 plus column within the block.
All inputs are finite; a program needn't handle non-finite values.
Results may differ from the reference program's by a relative error of at most 0.000096.
Values sent between devices are 32-bit elements; how exact they have to be, the bound alone decides.
A program may use at most 64 MiB of HBM per device.

```python
import math
import jax
import jax.numpy as jnp
from jax import lax

FEAT = 200
HID = 768
CH = 16
NPRED = 8
CX = 32
CY = 128
OBS_DEV = 2048
CAP = 64
NX = 128
NY = 1024
OBS_TOTAL = 65536
N_GY = 8
DEVICES = 32


def draw_obs_count(key, part):
    count_key, block_key = jax.random.split(jax.random.fold_in(key, 17))
    counts = jax.random.randint(count_key, (DEVICES, DEVICES), 0, CAP + 1)
    busy_block = jax.random.randint(block_key, (), 0, DEVICES)
    full_column = jnp.arange(DEVICES)[None, :] == busy_block
    return jnp.where(full_column, CAP, counts).astype(jnp.int32)


def touch_ends(entries, stream_key, least, high):
    longest = entries.shape.index(max(entries.shape))
    spots = []
    for shift in (0, 1):
        where = [jax.random.randint(jax.random.fold_in(stream_key, axis), (), 0, length) for axis, length in enumerate(entries.shape)]
        where[longest] = (where[longest] + shift) % entries.shape[longest]
        spots.append(tuple(where))
    return entries.at[spots[0]].set(least).at[spots[1]].set(high)


def block_levels(own_key, shape, pieces, smallest, largest):
    def one(dim, parts):
        draws = jax.random.uniform(jax.random.fold_in(jax.random.fold_in(own_key, 6), dim), (parts,), jnp.float32, smallest / len(pieces), largest / len(pieces))
        return jnp.repeat(jnp.exp(draws), shape[dim] // parts).reshape((-1,) + (1,) * (len(shape) - dim - 1))

    gain = one(*pieces[0])
    for cut in pieces[1:]:
        gain = gain * one(*cut)
    return gain


def noise(rng, extent, width, most, shards=(), kind=jnp.bfloat16):
    values = width * jax.random.normal(rng, extent, jnp.float32)
    if shards:
        values = values * block_levels(rng, extent, shards, -0.22, 0.18)
    return jnp.clip(values, -most, most).astype(kind)


def setup_inputs(seed: int = 0) -> dict:
    streams_of = jax.random.split(jax.random.key(seed), 14)
    return {
        "model_state": noise(streams_of[0], (FEAT, NX, NY), 1.0, 6.0, ((1, 4), (2, 8)), jnp.float32),
        "obs_cell": touch_ends(jax.random.randint(streams_of[1], (DEVICES, OBS_DEV), 0, CX * CY), jax.random.fold_in(streams_of[1], 1), 0, (CX * CY) - 1).astype(jnp.int32),
        "obs_count": draw_obs_count(jax.random.fold_in(streams_of[13], 71), 0),
        "obs_value": noise(streams_of[3], (CH, OBS_TOTAL), 1.0, 6.0, ((1, 32),), jnp.float32),
        "obs_weight": jnp.clip(jnp.exp(math.log(4.0) - 2.7725887 * jax.random.uniform(streams_of[4], (CH, OBS_TOTAL), jnp.float32) ** block_levels(streams_of[4], (CH, OBS_TOTAL), ((1, 32),), -0.2, 0.2)), 0.25, 4.0),
        "predictor": noise(streams_of[5], (NPRED, OBS_TOTAL), 1.0, 6.0, ((1, 32),), jnp.float32),
        "bias_coef": noise(streams_of[6], (CH, NPRED), 0.5, 3.0, (), jnp.float32),
        "weight_in": noise(streams_of[7], (HID, FEAT), FEAT ** -0.5, 0.4375, (), jnp.float32),
        "bias_in": noise(streams_of[8], (HID,), 0.5, 3.0, (), jnp.float32),
        "weight_mid": noise(streams_of[9], (HID, HID), HID ** -0.5, 0.21875, (), jnp.float32),
        "bias_mid": noise(streams_of[10], (HID,), 0.5, 3.0, (), jnp.float32),
        "weight_out": noise(streams_of[11], (CH, HID), HID ** -0.5, 0.21875, (), jnp.float32),
        "bias_out": noise(streams_of[12], (CH,), 1.0, 4.0, (), jnp.float32),
    }


def product(lhs_array, rhs_array):
    return jnp.dot(lhs_array, rhs_array, preferred_element_type=jnp.float32, precision=lax.Precision.HIGHEST)


def observe(profile, obs_rows, weight_rows, pred_rows, bias_coef, weight_in, bias_in, weight_mid, bias_mid, weight_out, bias_out):
    hidden_in = jnp.tanh(product(weight_in, profile) + bias_in[:, None])
    hidden_mid = jnp.tanh(product(weight_mid, hidden_in) + bias_mid[:, None])
    model_out = product(weight_out, hidden_mid) + bias_out[:, None] + product(bias_coef, pred_rows)
    residual_term = weight_rows * (model_out - obs_rows)
    back_mid = product(weight_out.T, residual_term) * (1.0 - hidden_mid * hidden_mid)
    back_in = product(weight_mid.T, back_mid) * (1.0 - hidden_in * hidden_in)
    increment = product(weight_in.T, back_in)
    bias_part = product(residual_term, pred_rows.T)
    return model_out, increment, bias_part


def reference(model_state, obs_cell, obs_count, obs_value, obs_weight, predictor, bias_coef, weight_in, bias_in, weight_mid, bias_mid, weight_out, bias_out):
    features = model_state.shape[0]
    flat_state = model_state.reshape(features, NX * NY)
    position = jnp.arange(OBS_DEV, dtype=jnp.int32)
    source = position // CAP
    base_row = (source // N_GY) * CX
    base_col = (source % N_GY) * CY
    global_cell = ((base_row[None, :] + obs_cell // CY) * NY + base_col[None, :] + obs_cell % CY).astype(jnp.int32)
    valid_slot = (jnp.arange(CAP, dtype=jnp.int32)[None, None, :] < obs_count[:, :, None]).reshape(DEVICES, OBS_DEV)
    value_blocks = obs_value.reshape(CH, DEVICES, OBS_DEV).transpose(1, 0, 2)
    weight_blocks = jnp.where(valid_slot[:, None, :], obs_weight.reshape(CH, DEVICES, OBS_DEV).transpose(1, 0, 2), jnp.float32(0.0))
    pred_blocks = predictor.reshape(NPRED, DEVICES, OBS_DEV).transpose(1, 0, 2)

    def owner_step(owner_items):
        cell_index, obs_rows, weight_rows, pred_rows = owner_items
        profile = jnp.take(flat_state, cell_index, axis=1)
        return observe(profile, obs_rows, weight_rows, pred_rows, bias_coef, weight_in, bias_in, weight_mid, bias_mid, weight_out, bias_out)

    model_out, increment, bias_part = lax.map(owner_step, (global_cell, value_blocks, weight_blocks, pred_blocks))
    evolved = jnp.where(valid_slot[:, None, :], model_out, jnp.float32(0.0)).transpose(1, 0, 2).reshape(CH, DEVICES * OBS_DEV)
    spread_back = increment.transpose(1, 0, 2).reshape(features, DEVICES * OBS_DEV)
    gradient = jnp.zeros((features, NX * NY), jnp.float32).at[:, global_cell.reshape(-1)].add(spread_back)
    return gradient.reshape(features, NX, NY), evolved, jnp.sum(bias_part, axis=0)
```

```python
import functools

import jax
import jax.numpy as jnp
from jax import lax
from jax.experimental import pallas as pl
from jax.experimental.pallas import tpu as pltpu
from jax.sharding import PartitionSpec as P

BF = jnp.bfloat16
F32 = jnp.float32


def round_up(value, step):
    return (value + step - 1) // step * step


def split_parts(x):
    hi = x.astype(BF)
    lo = (x - hi.astype(F32)).astype(BF)
    return hi, lo


def dot(a, b):
    return jnp.dot(a, b, preferred_element_type=F32)


def store_cat(ref, x, step):
    rows = x.shape[0]
    hi, lo = split_parts(x)
    ref[0:rows, :] = hi
    ref[step : step + rows, :] = lo
    ref[2 * step : 2 * step + rows, :] = hi


def weight_cat(ref, w, step):
    cols = w.shape[1]
    hi, lo = split_parts(w)
    ref[:, 0:cols] = hi
    ref[:, step : step + cols] = hi
    ref[:, 2 * step : 2 * step + cols] = lo


def prepare(w1t_ref, w2_ref, wo_ref, w1c, w1tc, w2c, w2tc, woc, wotc, pcat, rcat, padded, feat_pad):
    features, hid = w1t_ref.shape
    channels = wo_ref.shape[0]
    kp = padded.shape[0]
    padded[...] = jnp.zeros_like(padded)
    padded[0:features, :] = w1t_ref[...]
    weight_cat(w1tc, padded[0:feat_pad, :], hid)
    weight_cat(w1c, padded[...].T, kp)
    w2 = w2_ref[...]
    weight_cat(w2c, w2, hid)
    weight_cat(w2tc, w2.T, hid)
    wo = wo_ref[...]
    weight_cat(woc, wo, hid)
    hi = wo.astype(BF).astype(F32)
    padded[...] = jnp.zeros_like(padded)
    padded[0:channels, :] = hi
    padded[channels : 2 * channels, :] = hi
    padded[2 * channels : 3 * channels, :] = wo - hi
    wotc[...] = padded[0:128, :].T.astype(BF)
    pcat[...] = jnp.zeros_like(pcat)
    rcat[...] = jnp.zeros_like(rcat)


def split_state(st_ref, sp, features, feat_pad, block_rows):
    def body(r, carry):
        x = st_ref[pl.ds(r, features, stride=block_rows), :]
        if feat_pad > features:
            x = jnp.concatenate([x, jnp.zeros((feat_pad - features, x.shape[1]), F32)], axis=0)
        hi, lo = split_parts(x)
        at = pl.ds(pl.multiple_of(r * 128, 128), 128)
        sp[0:feat_pad, at] = hi
        sp[feat_pad : 2 * feat_pad, at] = lo
        return carry

    lax.fori_loop(0, block_rows, body, 0)


def build_onehot(cell, oh, at, block_rows, block_cols):
    n = cell.shape[1]
    row = jnp.floor(cell * (1.0 / block_cols))
    col = cell - row * block_cols
    lanes = lax.broadcasted_iota(jnp.int32, (block_cols, n), 0).astype(F32)
    colhot = jnp.where(lanes == col, 1.0, 0.0).astype(BF).reshape(block_cols // 16, 16, n)
    for r in range(block_rows):
        hit = jnp.broadcast_to(jnp.where(row == float(r), 1.0, 0.0), (16, n)).astype(BF)
        oh[r * block_cols : (r + 1) * block_cols, at] = (colhot * hit[None]).reshape(block_cols, n)


def compute_kernel(
    dims, in_ref, coef_ref, st_ref, w1t_ref, b1_ref, w2_ref, b2_ref, wo_ref, bo_ref,
    grad_ref, out_ref, bias_ref,
    w1c, w1tc, w2c, w2tc, woc, wotc, sp, oh, pcat, hcat, rcat, h1, h2, inc, res, padded,
):
    features, block_rows, block_cols, ts = dims
    hid = w2_ref.shape[0]
    channels = wo_ref.shape[0]
    preds = coef_ref.shape[1]
    feat_pad = sp.shape[0] // 2
    kp = padded.shape[0]
    slots = in_ref.shape[1]
    prepare(w1t_ref, w2_ref, wo_ref, w1c, w1tc, w2c, w2tc, woc, wotc, pcat, rcat, padded, feat_pad)
    split_state(st_ref, sp, features, feat_pad, block_rows)

    def chunk(t, carry):
        at = pl.ds(pl.multiple_of(t * ts, 128), ts)
        obs = in_ref[0:channels, at]
        wgt = in_ref[channels : 2 * channels, at]
        pred = in_ref[2 * channels : 2 * channels + preds, at]
        cell = in_ref[2 * channels + preds : 2 * channels + preds + 1, at]
        build_onehot(cell, oh, at, block_rows, block_cols)
        picked = dot(sp[...], oh[:, at]).astype(BF)
        pcat[0:feat_pad, :] = picked[0:feat_pad]
        pcat[kp : kp + feat_pad, :] = picked[feat_pad:]
        pcat[2 * kp : 2 * kp + feat_pad, :] = picked[0:feat_pad]
        a1 = jnp.tanh(dot(w1c[...], pcat[...]) + b1_ref[...])
        h1[...] = a1
        store_cat(hcat, a1, hid)
        a2 = jnp.tanh(dot(w2c[...], hcat[...]) + b2_ref[...])
        h2[...] = a2
        store_cat(hcat, a2, hid)
        model = dot(woc[...], hcat[...]) + bo_ref[...]
        for p in range(preds):
            model = model + coef_ref[:, p : p + 1] * pred[p : p + 1, :]
        out_ref[:, at] = model
        residual = wgt * (model - obs)
        res[:, at] = residual
        store_cat(rcat, residual, channels)
        a2 = h2[...]
        store_cat(hcat, dot(wotc[...], rcat[...]) * (1.0 - a2 * a2), hid)
        a1 = h1[...]
        store_cat(hcat, dot(w2tc[...], hcat[...]) * (1.0 - a1 * a1), hid)
        hi, lo = split_parts(dot(w1tc[...], hcat[...]))
        inc[0:feat_pad, at] = hi
        inc[feat_pad : 2 * feat_pad, at] = lo
        return carry

    lax.fori_loop(0, slots // ts, chunk, 0)
    bias_ref[...] = lax.dot_general(
        res[...], in_ref[2 * channels : 2 * channels + preds, :], (((1,), (1,)), ((), ())),
        preferred_element_type=F32, precision=lax.Precision.HIGHEST,
    )
    per = max(1, 256 // block_cols)

    def spread(q, carry):
        cells = pl.ds(pl.multiple_of(q * per * block_cols, 128), per * block_cols)
        got = lax.dot_general(
            inc[...], oh[cells, :], (((1,), (1,)), ((), ())), preferred_element_type=F32
        )
        total = got[0:features] + got[feat_pad : feat_pad + features]
        for k in range(per):
            grad_ref[pl.ds(q * per + k, features, stride=block_rows), :] = total[
                :, k * block_cols : (k + 1) * block_cols
            ]
        return carry

    lax.fori_loop(0, block_rows // per, spread, 0)


def run_compute(incoming, model_state, bias_coef, weight_in, bias_in, weight_mid, bias_mid, weight_out, bias_out):
    features, block_rows, block_cols = model_state.shape
    cells = block_rows * block_cols
    hid = weight_mid.shape[0]
    channels, preds = bias_coef.shape
    slots = incoming.shape[1]
    ts = 512
    fp = round_up(features, 16)
    kp = round_up(features, 256)
    vmem = pl.BlockSpec(memory_space=pltpu.VMEM)
    return pl.pallas_call(
        functools.partial(compute_kernel, (features, block_rows, block_cols, ts)),
        out_shape=(
            jax.ShapeDtypeStruct((features * block_rows, block_cols), F32),
            jax.ShapeDtypeStruct((channels, slots), F32),
            jax.ShapeDtypeStruct((channels, preds), F32),
        ),
        in_specs=[vmem] * 9,
        out_specs=(vmem,) * 3,
        scratch_shapes=[
            pltpu.VMEM((hid, 3 * kp), BF),
            pltpu.VMEM((fp, 3 * hid), BF),
            pltpu.VMEM((hid, 3 * hid), BF),
            pltpu.VMEM((hid, 3 * hid), BF),
            pltpu.VMEM((channels, 3 * hid), BF),
            pltpu.VMEM((hid, 128), BF),
            pltpu.VMEM((2 * fp, cells), BF),
            pltpu.VMEM((cells, slots), BF),
            pltpu.VMEM((3 * kp, ts), BF),
            pltpu.VMEM((3 * hid, ts), BF),
            pltpu.VMEM((128, ts), BF),
            pltpu.VMEM((hid, ts), F32),
            pltpu.VMEM((hid, ts), F32),
            pltpu.VMEM((2 * fp, slots), BF),
            pltpu.VMEM((channels, slots), F32),
            pltpu.VMEM((kp, hid), F32),
        ],
        compiler_params=pltpu.CompilerParams(vmem_limit_bytes=60 * 1024 * 1024),
        name="observe_block",
    )(
        incoming, bias_coef, model_state.reshape(features * block_rows, block_cols), weight_in.T,
        bias_in[:, None], weight_mid, bias_mid[:, None], weight_out, bias_out[:, None],
    )


def exchange_blocks(block_data):
    return lax.all_to_all(block_data, ("gx", "gy"), split_axis=1, concat_axis=1, tiled=True)


def per_device(
    model_state, obs_cell, obs_count, obs_value, obs_weight, predictor, bias_coef,
    weight_in, bias_in, weight_mid, bias_mid, weight_out, bias_out,
):
    devices = lax.axis_size("gx") * lax.axis_size("gy")
    slots = obs_cell.shape[1]
    capacity = slots // devices
    channels, preds = bias_coef.shape
    valid_slot = (
        jnp.arange(capacity, dtype=jnp.int32)[None, :] < obs_count[0][:, None]
    ).reshape(slots)
    masked_weight = jnp.where(valid_slot[None, :], obs_weight, jnp.float32(0.0))
    outgoing = jnp.concatenate(
        [obs_value, masked_weight, predictor, obs_cell.astype(F32)], axis=0
    )
    incoming = exchange_blocks(outgoing)
    gradient, local_out, bias_part = run_compute(
        incoming, model_state, bias_coef, weight_in, bias_in, weight_mid, bias_mid, weight_out, bias_out
    )
    back = jnp.concatenate(
        [
            local_out.reshape(channels, devices, capacity).transpose(1, 0, 2).reshape(devices, channels * capacity),
            jnp.broadcast_to(bias_part.reshape(1, channels * preds), (devices, channels * preds)),
        ],
        axis=1,
    )
    got = lax.all_to_all(back, ("gx", "gy"), split_axis=0, concat_axis=0, tiled=True)
    bias_gradient = jnp.sum(got[:, channels * capacity :], axis=0).reshape(channels, preds)
    model_out = (
        got[:, : channels * capacity].reshape(devices, channels, capacity).transpose(1, 0, 2).reshape(channels, slots)
    )
    evolved = jnp.where(valid_slot[None, :], model_out, jnp.float32(0.0))
    return (gradient.reshape(model_state.shape), evolved, bias_gradient)


def solution(mesh):
    split = ("gx", "gy")
    in_specs = (P(None, "gx", "gy"), P(split, None), P(split, None), P(None, split), P(None, split), P(None, split)) + (P(),) * 7
    out_specs = (P(None, "gx", "gy"), P(None, split), P())
    return jax.shard_map(per_device, mesh=mesh, in_specs=in_specs, out_specs=out_specs, check_vma=False)
```

```python
import functools

import jax
import jax.numpy as jnp
from jax import lax
from jax.experimental import pallas as pl
from jax.experimental.pallas import tpu as pltpu
from jax.sharding import PartitionSpec as P

BF = jnp.bfloat16
F32 = jnp.float32


def round_up(value, step):
    return (value + step - 1) // step * step


def split_parts(x):
    hi = x.astype(BF)
    lo = (x - hi.astype(F32)).astype(BF)
    return hi, lo


def dot(a, b):
    return jnp.dot(a, b, preferred_element_type=F32)


def store_cat(ref, x, step):
    rows = x.shape[0]
    hi, lo = split_parts(x)
    ref[0:rows, :] = hi
    ref[step : step + rows, :] = lo
    ref[2 * step : 2 * step + rows, :] = hi


def weight_cat(ref, w, step):
    cols = w.shape[1]
    hi, lo = split_parts(w)
    ref[:, 0:cols] = hi
    ref[:, step : step + cols] = hi
    ref[:, 2 * step : 2 * step + cols] = lo


def split_state(st_ref, sp, features, feat_pad, block_rows):
    def body(r, carry):
        x = st_ref[pl.ds(r, features, stride=block_rows), :]
        if feat_pad > features:
            x = jnp.concatenate([x, jnp.zeros((feat_pad - features, x.shape[1]), F32)], axis=0)
        hi, lo = split_parts(x)
        at = pl.ds(pl.multiple_of(r * 128, 128), 128)
        sp[0:feat_pad, at] = hi
        sp[feat_pad : 2 * feat_pad, at] = lo
        return carry

    lax.fori_loop(0, block_rows, body, 0)


def build_onehot(cell, oh, at, block_rows, block_cols):
    n = cell.shape[1]
    row = jnp.floor(cell * (1.0 / block_cols))
    col = cell - row * block_cols
    lanes = lax.broadcasted_iota(jnp.int32, (block_cols, n), 0).astype(F32)
    colhot = jnp.where(lanes == col, 1.0, 0.0).astype(BF).reshape(block_cols // 16, 16, n)
    for r in range(block_rows):
        hit = jnp.broadcast_to(jnp.where(row == float(r), 1.0, 0.0), (16, n)).astype(BF)
        oh[r * block_cols : (r + 1) * block_cols, at] = (colhot * hit[None]).reshape(block_cols, n)


MESH = pl.DeviceIdType.MESH


def prepare(w1t_ref, w2_ref, wo_ref, b1_ref, b2_ref, bo_ref, coeft_ref, w1c, w1tc, w2c, w2tc, woc, wotc, side, padded, feat_pad):
    features, hid = w1t_ref.shape
    channels = wo_ref.shape[0]
    preds = coeft_ref.shape[0]
    kp = padded.shape[0]
    padded[...] = jnp.zeros_like(padded)
    padded[0:features, :] = w1t_ref[...]
    weight_cat(w1tc, padded[0:feat_pad, :], hid)
    weight_cat(w1c, padded[...].T, kp)
    w2 = w2_ref[...]
    weight_cat(w2c, w2, hid)
    weight_cat(w2tc, w2.T, hid)
    wo = wo_ref[...]
    weight_cat(woc, wo, hid)
    hi = wo.astype(BF).astype(F32)
    base = 3 * channels
    padded[...] = jnp.zeros_like(padded)
    padded[0:channels, :] = hi
    padded[channels : 2 * channels, :] = hi
    padded[2 * channels : base, :] = wo - hi
    padded[base : base + 1, :] = b1_ref[...]
    padded[base + 1 : base + 2, :] = b2_ref[...]
    padded[base + 2 : base + 3, 0:channels] = bo_ref[...]
    padded[base + 8 : base + 8 + preds, 0:channels] = coeft_ref[...]
    turned = padded[0:128, :].T
    side[...] = turned
    wotc[...] = turned.astype(BF)


def fused_kernel(
    dims, cell_ref, cnt_ref, obs_ref, wgt_ref, pred_ref, coeft_ref, st_hbm, w1t_hbm, b1_ref, w2_hbm, b2_ref, wo_ref, bo_ref,
    grad_ref, evolved_ref, bias_ref,
    w1c, w1tc, w2c, w2tc, woc, wotc, sp, oh, pcat, hcat, rcat, h1, h2, inc, res, padded, side,
    st_ref, w1t_ref, w2_ref, cell_send, cell_recv, main_send, main_recv, out_send, out_recv, bias_send, bias_recv,
    incoming, load_sem, send_sem, recv_sem,
):
    features, block_rows, block_cols, ts, nx, ny = dims
    devices = nx * ny
    hid = w2_ref.shape[0]
    channels = wo_ref.shape[0]
    half = channels // 2
    preds = coeft_ref.shape[0]
    base = 3 * channels
    feat_pad = sp.shape[0] // 2
    kp = padded.shape[0]
    slots = obs_ref.shape[1]
    cap = slots // devices
    group = 128 // cap
    me = lax.axis_index("gx") * ny + lax.axis_index("gy")

    loads = [
        pltpu.make_async_copy(src, dst, load_sem.at[k])
        for k, (src, dst) in enumerate(((st_hbm, st_ref), (w1t_hbm, w1t_ref), (w2_hbm, w2_ref)))
    ]
    for load in loads:
        load.start()

    barrier = pltpu.get_barrier_semaphore()

    def greet(k, carry):
        peer = lax.rem(me + k, devices)
        pl.semaphore_signal(barrier, inc=1, device_id=(lax.div(peer, ny), lax.rem(peer, ny)), device_id_type=MESH)
        return carry

    lax.fori_loop(1, devices, greet, 0)

    lane = lax.broadcasted_iota(jnp.int32, (channels, 128), 1)
    lane8 = lax.broadcasted_iota(jnp.int32, (8, 128), 1)

    def turn(x, shift):
        shift = shift % 128
        return pltpu.roll(x, shift, 1) if shift else x

    def pack(g, carry):
        at = pl.ds(pl.multiple_of(g * 128, 128), 128)
        obs, wgt, pred = obs_ref[:, at], wgt_ref[:, at], pred_ref[:, at]
        cell = jnp.broadcast_to(cell_ref[:, at].astype(F32), (8, 128))
        for i in range(group):
            owner = g * group + i
            off = i * cap
            count = cnt_ref[0, owner]
            masked = jnp.where(lane - 64 < count, turn(wgt, 64 - off), 0.0)
            main_send[owner, 0:channels, :] = jnp.where(lane < 64, turn(obs, -off), masked)
            main_send[owner, channels : channels + preds, :] = turn(pred, -off)
            cell_send[owner] = turn(cell, -off)[0:1]
        return carry

    lax.fori_loop(0, slots // 128, pack, 0)
    pl.semaphore_wait(barrier, devices - 1)

    def remote(src, dst, kind, peer):
        return pltpu.make_async_remote_copy(
            src_ref=src, dst_ref=dst, send_sem=send_sem.at[kind], recv_sem=recv_sem.at[kind],
            device_id=(lax.div(peer, ny), lax.rem(peer, ny)), device_id_type=MESH,
        )

    def send_cells(k, carry):
        peer = lax.rem(me + k, devices)
        remote(cell_send.at[peer], cell_recv.at[me], 0, peer).start()
        return carry

    def send_main(k, carry):
        peer = lax.rem(me + k, devices)
        remote(main_send.at[peer], main_recv.at[me], 1, peer).start()
        return carry

    lax.fori_loop(1, devices, send_cells, 0)
    lax.fori_loop(1, devices, send_main, 0)
    cell_recv[me] = cell_send[me]
    main_recv[me] = main_send[me]

    def wait_all(ref, sem):
        part = ref.at[pl.ds(0, devices - 1)]
        pltpu.make_async_copy(part, part, sem).wait()

    loads[1].wait()
    loads[2].wait()
    prepare(w1t_ref, w2_ref, wo_ref, b1_ref, b2_ref, bo_ref, coeft_ref, w1c, w1tc, w2c, w2tc, woc, wotc, side, padded, feat_pad)
    pcat[...] = jnp.zeros_like(pcat)
    rcat[...] = jnp.zeros_like(rcat)
    loads[0].wait()
    split_state(st_ref, sp, features, feat_pad, block_rows)
    wait_all(cell_recv, recv_sem.at[0])

    def chunk(t, carry):
        at = pl.ds(pl.multiple_of(t * ts, 128), ts)
        first = t * (ts // cap)
        tiles = []
        for g in range(ts // 128):
            row = jnp.zeros((8, 128), F32)
            for i in range(group):
                piece = jnp.broadcast_to(cell_recv[first + g * group + i], (8, 128))
                here = (lane8 >= i * cap) & (lane8 < (i + 1) * cap)
                row = jnp.where(here, turn(piece, i * cap), row)
            tiles.append(row)
        cell = jnp.concatenate(tiles, axis=1)[0:1]
        build_onehot(cell, oh, at, block_rows, block_cols)
        picked = dot(sp[...], oh[:, at]).astype(BF)
        pcat[0:feat_pad, :] = picked[0:feat_pad]
        pcat[kp : kp + feat_pad, :] = picked[feat_pad:]
        pcat[2 * kp : 2 * kp + feat_pad, :] = picked[0:feat_pad]
        a1 = jnp.tanh(dot(w1c[...], pcat[...]) + side[:, base : base + 1])
        h1[...] = a1
        store_cat(hcat, a1, hid)
        a2 = jnp.tanh(dot(w2c[...], hcat[...]) + side[:, base + 1 : base + 2])
        h2[...] = a2
        store_cat(hcat, a2, hid)

        @pl.when(t == 0)
        def _():
            wait_all(main_recv, recv_sem.at[1])

        for g in range(ts // 128):
            spot = slice(g * 128, (g + 1) * 128)
            value = jnp.zeros((channels, 128), F32)
            weight = jnp.zeros((channels, 128), F32)
            factor = jnp.zeros((preds, 128), F32)
            for i in range(group):
                got = main_recv[first + g * group + i]
                here = (lane >= i * cap) & (lane < (i + 1) * cap)
                value = jnp.where(here, turn(got[0:channels], i * cap), value)
                weight = jnp.where(here, turn(got[0:channels], i * cap - 64), weight)
                factor = jnp.where(here[0:preds], turn(got[channels : channels + preds], i * cap), factor)
            incoming[t, 0:channels, spot] = value
            incoming[t, channels : 2 * channels, spot] = weight
            incoming[t, 2 * channels : 2 * channels + preds, spot] = factor
        obs = incoming[t, 0:channels, :]
        wgt = incoming[t, channels : 2 * channels, :]
        pred = incoming[t, 2 * channels : 2 * channels + preds, :]
        model = dot(woc[...], hcat[...]) + side[0:channels, base + 2 : base + 3]
        for p in range(preds):
            model = model + side[0:channels, base + 8 + p : base + 9 + p] * pred[p : p + 1, :]
        residual = wgt * (model - obs)
        res[t] = residual
        for g in range(ts // 128):
            spot = slice(g * 128, (g + 1) * 128)
            upper, lower = model[0:half, spot], model[half:, spot]
            for i in range(group):
                out_send[first + g * group + i] = jnp.where(
                    lane8 < 64, turn(upper, -i * cap), turn(lower, 64 - i * cap)
                )

        def give_back(n, carry):
            peer = first + n

            @pl.when(peer != me)
            def _():
                remote(out_send.at[peer], out_recv.at[me], 2, peer).start()

            return carry

        lax.fori_loop(0, ts // cap, give_back, 0)
        store_cat(rcat, residual, channels)
        a2 = h2[...]
        store_cat(hcat, dot(wotc[...], rcat[...]) * (1.0 - a2 * a2), hid)
        a1 = h1[...]
        store_cat(hcat, dot(w2tc[...], hcat[...]) * (1.0 - a1 * a1), hid)
        hi, lo = split_parts(dot(w1tc[...], hcat[...]))
        inc[0:feat_pad, at] = hi
        inc[feat_pad : 2 * feat_pad, at] = lo
        return carry

    lax.fori_loop(0, slots // ts, chunk, 0)
    out_recv[me] = out_send[me]
    terms = jnp.zeros((preds, channels), F32)
    for t in range(slots // ts):
        terms = terms + lax.dot_general(
            incoming[t, 2 * channels : 2 * channels + preds, :], res[t], (((1,), (1,)), ((), ())),
            preferred_element_type=F32, precision=lax.Precision.HIGHEST,
        )
    bias_send[...] = jnp.zeros_like(bias_send)
    bias_send[:, 0:channels] = terms
    bias_recv[me] = bias_send[...]

    def send_bias(k, carry):
        peer = lax.rem(me + k, devices)
        remote(bias_send, bias_recv.at[me], 3, peer).start()
        return carry

    lax.fori_loop(1, devices, send_bias, 0)
    per = max(1, 256 // block_cols)

    def spread(q, carry):
        cells = pl.ds(pl.multiple_of(q * per * block_cols, 128), per * block_cols)
        got = lax.dot_general(
            inc[...], oh[cells, :], (((1,), (1,)), ((), ())), preferred_element_type=F32
        )
        total = got[0:features] + got[feat_pad : feat_pad + features]
        for k in range(per):
            grad_ref[pl.ds(q * per + k, features, stride=block_rows), :] = total[
                :, k * block_cols : (k + 1) * block_cols
            ]
        return carry

    lax.fori_loop(0, block_rows // per, spread, 0)
    wait_all(out_recv, recv_sem.at[2])

    def finish(g, carry):
        at = pl.ds(pl.multiple_of(g * 128, 128), 128)
        upper = jnp.zeros((half, 128), F32)
        lower = jnp.zeros((half, 128), F32)
        for i in range(group):
            block = g * group + i
            got = out_recv[block]
            here = (lane8 >= i * cap) & (lane8 < i * cap + jnp.minimum(cnt_ref[0, block], cap))
            upper = jnp.where(here, turn(got, i * cap), upper)
            lower = jnp.where(here, turn(got, i * cap - 64), lower)
        evolved_ref[0:half, at] = upper
        evolved_ref[half:channels, at] = lower
        return carry

    lax.fori_loop(0, slots // 128, finish, 0)
    wait_all(bias_recv, recv_sem.at[3])
    bias_ref[...] = jnp.sum(bias_recv[...], axis=0)[:, 0:channels]
    wait_all(cell_send, send_sem.at[0])
    wait_all(main_send, send_sem.at[1])
    wait_all(out_send, send_sem.at[2])
    wait_all(bias_recv, send_sem.at[3])


def per_device(
    nx, ny, model_state, obs_cell, obs_count, obs_value, obs_weight, predictor, bias_coef,
    weight_in, bias_in, weight_mid, bias_mid, weight_out, bias_out,
):
    features, block_rows, block_cols = model_state.shape
    cells = block_rows * block_cols
    hid = weight_mid.shape[0]
    channels, preds = bias_coef.shape
    slots = obs_value.shape[1]
    devices = nx * ny
    ts = min(512, slots)
    fp = round_up(features, 16)
    kp = round_up(features, 256)
    vmem = pl.BlockSpec(memory_space=pltpu.VMEM)
    hbm = pl.BlockSpec(memory_space=pl.ANY)
    smem = pl.BlockSpec(memory_space=pltpu.SMEM)
    rows = channels + preds
    gradient, evolved, bias = pl.pallas_call(
        functools.partial(fused_kernel, (features, block_rows, block_cols, ts, nx, ny)),
        out_shape=(
            jax.ShapeDtypeStruct((features * block_rows, block_cols), F32),
            jax.ShapeDtypeStruct((channels, slots), F32),
            jax.ShapeDtypeStruct((preds, channels), F32),
        ),
        in_specs=[vmem, smem, vmem, vmem, vmem, vmem, hbm, hbm, vmem, hbm, vmem, vmem, vmem],
        out_specs=(vmem,) * 3,
        scratch_shapes=[
            pltpu.VMEM((hid, 3 * kp), BF),
            pltpu.VMEM((fp, 3 * hid), BF),
            pltpu.VMEM((hid, 3 * hid), BF),
            pltpu.VMEM((hid, 3 * hid), BF),
            pltpu.VMEM((channels, 3 * hid), BF),
            pltpu.VMEM((hid, 128), BF),
            pltpu.VMEM((2 * fp, cells), BF),
            pltpu.VMEM((cells, slots), BF),
            pltpu.VMEM((3 * kp, ts), BF),
            pltpu.VMEM((3 * hid, ts), BF),
            pltpu.VMEM((128, ts), BF),
            pltpu.VMEM((hid, ts), F32),
            pltpu.VMEM((hid, ts), F32),
            pltpu.VMEM((2 * fp, slots), BF),
            pltpu.VMEM((slots // ts, channels, ts), F32),
            pltpu.VMEM((kp, hid), F32),
            pltpu.VMEM((hid, 128), F32),
            pltpu.VMEM((features * block_rows, block_cols), F32),
            pltpu.VMEM((features, hid), F32),
            pltpu.VMEM((hid, hid), F32),
            pltpu.VMEM((devices, 1, 128), F32),
            pltpu.VMEM((devices, 1, 128), F32),
            pltpu.VMEM((devices, rows, 128), F32),
            pltpu.VMEM((devices, rows, 128), F32),
            pltpu.VMEM((devices, channels // 2, 128), F32),
            pltpu.VMEM((devices, channels // 2, 128), F32),
            pltpu.VMEM((preds, 128), F32),
            pltpu.VMEM((devices, preds, 128), F32),
            pltpu.VMEM((slots // ts, 2 * channels + preds, ts), F32),
            pltpu.SemaphoreType.DMA((3,)),
            pltpu.SemaphoreType.DMA((4,)),
            pltpu.SemaphoreType.DMA((4,)),
        ],
        compiler_params=pltpu.CompilerParams(
            vmem_limit_bytes=60 * 1024 * 1024, collective_id=0, has_side_effects=True
        ),
        name="observe_all",
    )(
        obs_cell, obs_count, obs_value, obs_weight, predictor, bias_coef.T,
        model_state.reshape(features * block_rows, block_cols), weight_in.T,
        bias_in[None, :], weight_mid, bias_mid[None, :], weight_out, bias_out[None, :],
    )
    return (gradient.reshape(model_state.shape), evolved, bias.T)


def solution(mesh):
    split = ("gx", "gy")
    in_specs = (P(None, "gx", "gy"), P(split, None), P(split, None), P(None, split), P(None, split), P(None, split)) + (P(),) * 7
    out_specs = (P(None, "gx", "gy"), P(None, split), P())
    local = functools.partial(per_device, mesh.shape["gx"], mesh.shape["gy"])
    return jax.shard_map(local, mesh=mesh, in_specs=in_specs, out_specs=out_specs, check_vma=False)
```

```python
import functools

import jax
import jax.numpy as jnp
from jax import lax
from jax.experimental import pallas as pl
from jax.experimental.pallas import tpu as pltpu
from jax.sharding import PartitionSpec as P

BF = jnp.bfloat16
F32 = jnp.float32


def round_up(value, step):
    return (value + step - 1) // step * step


def split_parts(x):
    hi = x.astype(BF)
    lo = (x - hi.astype(F32)).astype(BF)
    return hi, lo


def dot(a, b):
    return jnp.dot(a, b, preferred_element_type=F32)


def store_cat(ref, x, step):
    rows = x.shape[0]
    hi, lo = split_parts(x)
    ref[0:rows, :] = hi
    ref[step : step + rows, :] = lo
    ref[2 * step : 2 * step + rows, :] = hi


def weight_cat(ref, w, step):
    cols = w.shape[1]
    hi, lo = split_parts(w)
    ref[:, 0:cols] = hi
    ref[:, step : step + cols] = hi
    ref[:, 2 * step : 2 * step + cols] = lo


def split_state(st_ref, sp, features, feat_pad, block_rows):
    def body(r, carry):
        x = st_ref[pl.ds(r, features, stride=block_rows), :]
        if feat_pad > features:
            x = jnp.concatenate([x, jnp.zeros((feat_pad - features, x.shape[1]), F32)], axis=0)
        hi, lo = split_parts(x)
        at = pl.ds(pl.multiple_of(r * 128, 128), 128)
        sp[0:feat_pad, at] = hi
        sp[feat_pad : 2 * feat_pad, at] = lo
        return carry

    lax.fori_loop(0, block_rows, body, 0)


def build_onehot(cell, oh, at, block_rows, block_cols):
    n = cell.shape[1]
    row = jnp.floor(cell * (1.0 / block_cols))
    col = cell - row * block_cols
    lanes = lax.broadcasted_iota(jnp.int32, (block_cols, n), 0).astype(F32)
    colhot = jnp.where(lanes == col, 1.0, 0.0).astype(BF).reshape(block_cols // 16, 16, n)
    for r in range(block_rows):
        hit = jnp.broadcast_to(jnp.where(row == float(r), 1.0, 0.0), (16, n)).astype(BF)
        oh[r * block_cols : (r + 1) * block_cols, at] = (colhot * hit[None]).reshape(block_cols, n)


MESH = pl.DeviceIdType.MESH


def prepare(w1t_ref, w2_ref, wo_ref, b1_ref, b2_ref, bo_ref, coeft_ref, w1c, w1tc, w2c, w2tc, woc, wotc, side, padded, feat_pad):
    features, hid = w1t_ref.shape
    channels = wo_ref.shape[0]
    preds = coeft_ref.shape[0]
    kp = padded.shape[0]
    padded[...] = jnp.zeros_like(padded)
    padded[0:features, :] = w1t_ref[...]
    weight_cat(w1tc, padded[0:feat_pad, :], hid)
    weight_cat(w1c, padded[...].T, kp)
    w2 = w2_ref[...]
    weight_cat(w2c, w2, hid)
    weight_cat(w2tc, w2.T, hid)
    wo = wo_ref[...]
    weight_cat(woc, wo, hid)
    hi = wo.astype(BF).astype(F32)
    base = 3 * channels
    padded[...] = jnp.zeros_like(padded)
    padded[0:channels, :] = hi
    padded[channels : 2 * channels, :] = hi
    padded[2 * channels : base, :] = wo - hi
    padded[base : base + 1, :] = b1_ref[...].reshape(1, hid)
    padded[base + 1 : base + 2, :] = b2_ref[...].reshape(1, hid)
    padded[base + 2 : base + 3, 0:channels] = bo_ref[...]
    padded[base + 8 : base + 8 + preds, 0:channels] = coeft_ref[...]
    turned = padded[0:128, :].T
    side[...] = turned
    wotc[...] = turned.astype(BF)


def fused_kernel(
    dims, cell_ref, cnt_ref, obs_ref, wgt_ref, pred_ref, coeft_ref, st_hbm, w1t_hbm, b1_ref, w2_hbm, b2_ref, wo_ref, bo_ref,
    inc, cells_ref, evolved_ref, bias_ref,
    w1c, w1tc, w2c, w2tc, woc, wotc, sp, oh, pcats, hcats, gcats, rcats, h1s, h2s, terms_ref, padded, side,
    st_ref, w1t_ref, w2_ref, cell_send, cell_recv, main_send, main_recv, out_send, out_recv, bias_send, bias_recv,
    incoming, load_sem, send_sem, recv_sem,
):
    features, block_rows, block_cols, ts, nx, ny = dims
    devices = nx * ny
    hid = w2_ref.shape[0]
    channels = wo_ref.shape[0]
    half = channels // 2
    preds = coeft_ref.shape[0]
    base = 3 * channels
    feat_pad = sp.shape[0] // 2
    kp = padded.shape[0]
    slots = obs_ref.shape[1]
    cap = slots // devices
    group = 128 // cap
    me = lax.axis_index("gx") * ny + lax.axis_index("gy")

    loads = [
        pltpu.make_async_copy(src, dst, load_sem.at[k])
        for k, (src, dst) in enumerate(((st_hbm, st_ref), (w1t_hbm, w1t_ref), (w2_hbm, w2_ref)))
    ]
    for load in loads:
        load.start()

    barrier = pltpu.get_barrier_semaphore()

    def greet(k, carry):
        peer = lax.rem(me + k, devices)
        pl.semaphore_signal(barrier, inc=1, device_id=(lax.div(peer, ny), lax.rem(peer, ny)), device_id_type=MESH)
        return carry

    lax.fori_loop(1, devices, greet, 0)

    lane = lax.broadcasted_iota(jnp.int32, (channels, 128), 1)
    lane8 = lax.broadcasted_iota(jnp.int32, (8, 128), 1)

    def turn(x, shift):
        shift = shift % 128
        return pltpu.roll(x, shift, 1) if shift else x

    def pack(g, carry):
        at = pl.ds(pl.multiple_of(g * 128, 128), 128)
        obs, wgt, pred = obs_ref[:, at], wgt_ref[:, at], pred_ref[:, at]
        for i in range(group):
            owner = g * group + i
            off = i * cap
            count = cnt_ref[0, owner]
            masked = jnp.where(lane - 64 < count, turn(wgt, 64 - off), 0.0)
            main_send[owner, 0:channels, :] = jnp.where(lane < 64, turn(obs, -off), masked)
            main_send[owner, channels : channels + preds, :] = turn(pred, -off)
        return carry

    def pack_cells(g, carry):
        at = pl.ds(pl.multiple_of(g * 128, 128), 128)
        cell = jnp.broadcast_to(cell_ref[:, at].astype(F32), (8, 128))
        for i in range(group):
            cell_send[g * group + i] = turn(cell, -i * cap)[0:1]
        return carry

    lax.fori_loop(0, slots // 128, pack_cells, 0)
    pl.semaphore_wait(barrier, devices - 1)

    def remote(src, dst, kind, peer):
        return pltpu.make_async_remote_copy(
            src_ref=src, dst_ref=dst, send_sem=send_sem.at[kind], recv_sem=recv_sem.at[kind],
            device_id=(lax.div(peer, ny), lax.rem(peer, ny)), device_id_type=MESH,
        )

    def send_cells(k, carry):
        peer = lax.rem(me + k, devices)
        remote(cell_send.at[peer], cell_recv.at[me], 0, peer).start()
        return carry

    def send_main(k, carry):
        peer = lax.rem(me + k, devices)
        remote(main_send.at[peer], main_recv.at[me], 1, peer).start()
        return carry

    lax.fori_loop(1, devices, send_cells, 0)
    lax.fori_loop(0, slots // 128, pack, 0)
    lax.fori_loop(1, devices, send_main, 0)
    cell_recv[me] = cell_send[me]
    main_recv[me] = main_send[me]

    def wait_all(ref, sem):
        part = ref.at[pl.ds(0, devices - 1)]
        pltpu.make_async_copy(part, part, sem).wait()

    loads[1].wait()
    loads[2].wait()
    prepare(w1t_ref, w2_ref, wo_ref, b1_ref, b2_ref, bo_ref, coeft_ref, w1c, w1tc, w2c, w2tc, woc, wotc, side, padded, feat_pad)
    pcats[...] = jnp.zeros_like(pcats)
    rcats[...] = jnp.zeros_like(rcats)
    terms_ref[...] = jnp.zeros_like(terms_ref)
    loads[0].wait()
    split_state(st_ref, sp, features, feat_pad, block_rows)
    wait_all(cell_recv, recv_sem.at[0])

    def send_bias(k, carry):
        peer = lax.rem(me + k, devices)
        remote(bias_send, bias_recv.at[me], 3, peer).start()
        return carry

    def chunk(t, carry):
        at = pl.ds(pl.multiple_of(t * ts, 128), ts)
        first = t * (ts // cap)
        tiles = []
        for g in range(ts // 128):
            row = jnp.zeros((8, 128), F32)
            for i in range(group):
                piece = jnp.broadcast_to(cell_recv[first + g * group + i], (8, 128))
                here = (lane8 >= i * cap) & (lane8 < (i + 1) * cap)
                row = jnp.where(here, turn(piece, i * cap), row)
            tiles.append(row)
        cell = jnp.concatenate(tiles, axis=1)[0:1]
        cells_ref[:, at] = cell
        build_onehot(cell, oh, slice(0, ts), block_rows, block_cols)
        sub = ts // 2
        sides = (0, 1)
        for u in sides:
            picked = dot(sp[...], oh[:, u * sub : (u + 1) * sub]).astype(BF)
            pcats[u, 0:feat_pad, :] = picked[0:feat_pad]
            pcats[u, kp : kp + feat_pad, :] = picked[feat_pad:]
            pcats[u, 2 * kp : 2 * kp + feat_pad, :] = picked[0:feat_pad]
        for u in sides:
            a1 = jnp.tanh(dot(w1c[...], pcats[u]) + side[:, base : base + 1])
            h1s[u] = a1
            store_cat(hcats.at[u], a1, hid)
        for u in sides:
            a2 = jnp.tanh(dot(w2c[...], hcats[u]) + side[:, base + 1 : base + 2])
            h2s[u] = a2
            store_cat(gcats.at[u], a2, hid)
        heads = [dot(woc[...], gcats[u]) for u in sides]

        @pl.when(t == 0)
        def _():
            wait_all(main_recv, recv_sem.at[1])

        for g in range(ts // 128):
            spot = slice(g * 128, (g + 1) * 128)
            value = jnp.zeros((channels, 128), F32)
            weight = jnp.zeros((channels, 128), F32)
            factor = jnp.zeros((preds, 128), F32)
            for i in range(group):
                got = main_recv[first + g * group + i]
                here = (lane >= i * cap) & (lane < (i + 1) * cap)
                value = jnp.where(here, turn(got[0:channels], i * cap), value)
                weight = jnp.where(here, turn(got[0:channels], i * cap - 64), weight)
                factor = jnp.where(here[0:preds], turn(got[channels : channels + preds], i * cap), factor)
            incoming[t, 0:channels, spot] = value
            incoming[t, channels : 2 * channels, spot] = weight
            incoming[t, 2 * channels : 2 * channels + preds, spot] = factor
        obs = incoming[t, 0:channels, :]
        wgt = incoming[t, channels : 2 * channels, :]
        pred = incoming[t, 2 * channels : 2 * channels + preds, :]
        model = jnp.concatenate(heads, axis=1) + side[0:channels, base + 2 : base + 3]
        for p in range(preds):
            model = model + side[0:channels, base + 8 + p : base + 9 + p] * pred[p : p + 1, :]
        residual = wgt * (model - obs)
        terms_ref[:, 0:channels] += lax.dot_general(
            pred, residual, (((1,), (1,)), ((), ())),
            preferred_element_type=F32, precision=lax.Precision.HIGHEST,
        )
        for g in range(ts // 128):
            spot = slice(g * 128, (g + 1) * 128)
            upper, lower = model[0:half, spot], model[half:, spot]
            for i in range(group):
                out_send[first + g * group + i] = jnp.where(
                    lane8 < 64, turn(upper, -i * cap), turn(lower, 64 - i * cap)
                )

        def give_back(n, carry):
            peer = first + n

            @pl.when(peer != me)
            def _():
                remote(out_send.at[peer], out_recv.at[me], 2, peer).start()

            return carry

        lax.fori_loop(0, ts // cap, give_back, 0)

        @pl.when(t == slots // ts - 1)
        def _():
            bias_send[...] = terms_ref[...]
            lax.fori_loop(1, devices, send_bias, 0)

        for u in sides:
            store_cat(rcats.at[u], residual[:, u * sub : (u + 1) * sub], channels)
        for u in sides:
            a2 = h2s[u]
            store_cat(hcats.at[u], dot(wotc[...], rcats[u]) * (1.0 - a2 * a2), hid)
        for u in sides:
            a1 = h1s[u]
            store_cat(gcats.at[u], dot(w2tc[...], hcats[u]) * (1.0 - a1 * a1), hid)
        for u in sides:
            hi, lo = split_parts(dot(w1tc[...], gcats[u]))
            here = pl.ds(pl.multiple_of(t * ts + u * sub, 128), sub)
            inc[0:feat_pad, here] = hi
            inc[feat_pad : 2 * feat_pad, here] = lo
        return carry

    lax.fori_loop(0, slots // ts, chunk, 0)
    out_recv[me] = out_send[me]
    bias_recv[me] = bias_send[...]
    wait_all(out_recv, recv_sem.at[2])

    def finish(g, carry):
        at = pl.ds(pl.multiple_of(g * 128, 128), 128)
        upper = jnp.zeros((half, 128), F32)
        lower = jnp.zeros((half, 128), F32)
        for i in range(group):
            block = g * group + i
            got = out_recv[block]
            here = (lane8 >= i * cap) & (lane8 < i * cap + jnp.minimum(cnt_ref[0, block], cap))
            upper = jnp.where(here, turn(got, i * cap), upper)
            lower = jnp.where(here, turn(got, i * cap - 64), lower)
        evolved_ref[0:half, at] = upper
        evolved_ref[half:channels, at] = lower
        return carry

    lax.fori_loop(0, slots // 128, finish, 0)
    wait_all(bias_recv, recv_sem.at[3])
    bias_ref[...] = jnp.sum(bias_recv[...], axis=0)[:, 0:channels]
    wait_all(cell_send, send_sem.at[0])
    wait_all(main_send, send_sem.at[1])
    wait_all(out_send, send_sem.at[2])
    wait_all(bias_recv, send_sem.at[3])


def spread_kernel(inc_ref, cells_ref, grad_ref, colhot, oh):
    features, row_step, block_cols = grad_ref.shape
    feat_pad = inc_ref.shape[0] // 2
    n = inc_ref.shape[1]
    step = pl.program_id(0)
    cell = cells_ref[...]
    row = jnp.floor(cell * (1.0 / block_cols))

    @pl.when(step == 0)
    def _():
        lanes = lax.broadcasted_iota(jnp.int32, (block_cols, n), 0).astype(F32)
        colhot[...] = jnp.where(lanes == cell - row * block_cols, 1.0, 0.0).astype(BF)

    away = row - (step * row_step).astype(F32)
    per = max(1, 256 // block_cols)
    for q in range(row_step // per):
        for k in range(per):
            hit = jnp.where(away == float(q * per + k), 1.0, 0.0)
            hit = jnp.broadcast_to(hit, (16, n)).astype(BF)
            part = colhot[...].reshape(block_cols // 16, 16, n) * hit[None]
            oh[q, k * block_cols : (k + 1) * block_cols, :] = part.reshape(block_cols, n)
    for q in range(row_step // per):
        got = lax.dot_general(
            inc_ref[...], oh[q], (((1,), (1,)), ((), ())), preferred_element_type=F32
        )
        total = got[0:features] + got[feat_pad : feat_pad + features]
        for k in range(per):
            grad_ref[:, q * per + k, :] = total[:, k * block_cols : (k + 1) * block_cols]


def per_device(
    nx, ny, model_state, obs_cell, obs_count, obs_value, obs_weight, predictor, bias_coef,
    weight_in, bias_in, weight_mid, bias_mid, weight_out, bias_out,
):
    features, block_rows, block_cols = model_state.shape
    cells = block_rows * block_cols
    hid = weight_mid.shape[0]
    channels, preds = bias_coef.shape
    slots = obs_value.shape[1]
    devices = nx * ny
    ts = min(512, slots)
    fp = round_up(features, 16)
    kp = round_up(features, 256)
    vmem = pl.BlockSpec(memory_space=pltpu.VMEM)
    hbm = pl.BlockSpec(memory_space=pl.ANY)
    smem = pl.BlockSpec(memory_space=pltpu.SMEM)
    rows = channels + preds
    parts, chosen, evolved, bias = pl.pallas_call(
        functools.partial(fused_kernel, (features, block_rows, block_cols, ts, nx, ny)),
        out_shape=(
            jax.ShapeDtypeStruct((2 * fp, slots), BF),
            jax.ShapeDtypeStruct((1, slots), F32),
            jax.ShapeDtypeStruct((channels, slots), F32),
            jax.ShapeDtypeStruct((preds, channels), F32),
        ),
        in_specs=[vmem, smem, vmem, vmem, vmem, vmem, hbm, hbm, vmem, hbm, vmem, vmem, vmem],
        out_specs=(vmem,) * 4,
        scratch_shapes=[
            pltpu.VMEM((hid, 3 * kp), BF),
            pltpu.VMEM((fp, 3 * hid), BF),
            pltpu.VMEM((hid, 3 * hid), BF),
            pltpu.VMEM((hid, 3 * hid), BF),
            pltpu.VMEM((channels, 3 * hid), BF),
            pltpu.VMEM((hid, 128), BF),
            pltpu.VMEM((2 * fp, cells), BF),
            pltpu.VMEM((cells, ts), BF),
            pltpu.VMEM((2, 3 * kp, ts // 2), BF),
            pltpu.VMEM((2, 3 * hid, ts // 2), BF),
            pltpu.VMEM((2, 3 * hid, ts // 2), BF),
            pltpu.VMEM((2, 128, ts // 2), BF),
            pltpu.VMEM((2, hid, ts // 2), F32),
            pltpu.VMEM((2, hid, ts // 2), F32),
            pltpu.VMEM((preds, 128), F32),
            pltpu.VMEM((kp, hid), F32),
            pltpu.VMEM((hid, 128), F32),
            pltpu.VMEM((features * block_rows, block_cols), F32),
            pltpu.VMEM((features, hid), F32),
            pltpu.VMEM((hid, hid), F32),
            pltpu.VMEM((devices, 1, 128), F32),
            pltpu.VMEM((devices, 1, 128), F32),
            pltpu.VMEM((devices, rows, 128), F32),
            pltpu.VMEM((devices, rows, 128), F32),
            pltpu.VMEM((devices, channels // 2, 128), F32),
            pltpu.VMEM((devices, channels // 2, 128), F32),
            pltpu.VMEM((preds, 128), F32),
            pltpu.VMEM((devices, preds, 128), F32),
            pltpu.VMEM((slots // ts, 2 * channels + preds, ts), F32),
            pltpu.SemaphoreType.DMA((3,)),
            pltpu.SemaphoreType.DMA((4,)),
            pltpu.SemaphoreType.DMA((4,)),
        ],
        compiler_params=pltpu.CompilerParams(
            vmem_limit_bytes=60 * 1024 * 1024, collective_id=0, has_side_effects=True
        ),
        name="observe_all",
    )(
        obs_cell, obs_count, obs_value, obs_weight, predictor, bias_coef.T,
        model_state.reshape(features * block_rows, block_cols), weight_in.T,
        bias_in, weight_mid, bias_mid, weight_out, bias_out[None, :],
    )
    row_step = min(8, block_rows)
    gradient = pl.pallas_call(
        spread_kernel,
        grid=(block_rows // row_step,),
        out_shape=jax.ShapeDtypeStruct(model_state.shape, F32),
        in_specs=[vmem, vmem],
        out_specs=pl.BlockSpec((features, row_step, block_cols), lambda g: (0, g, 0)),
        scratch_shapes=[
            pltpu.VMEM((block_cols, slots), BF),
            pltpu.VMEM((row_step * block_cols // 256, 256, slots), BF),
        ],
        compiler_params=pltpu.CompilerParams(vmem_limit_bytes=48 * 1024 * 1024),
        name="spread_increments",
    )(parts, chosen)
    return (gradient, evolved, bias.T)


def solution(mesh):
    split = ("gx", "gy")
    in_specs = (P(None, "gx", "gy"), P(split, None), P(split, None), P(None, split), P(None, split), P(None, split)) + (P(),) * 7
    out_specs = (P(None, "gx", "gy"), P(None, split), P())
    local = functools.partial(per_device, mesh.shape["gx"], mesh.shape["gy"])
    return jax.shard_map(local, mesh=mesh, in_specs=in_specs, out_specs=out_specs, check_vma=False)
```
